32 devices in a mesh: seq: 8 (over z, y), head: 4 (over x, core).
Axes of the slice: x: 2, y: 2, z: 4, core: 2. Of those that a mesh axis runs over, the one named last changes fastest.
Arguments:
- tokens: bfloat16 [2, 1024, 2560], P(None, 'seq', 'head'), may hold values from -6 to 6
- token_mix: float32 [5, 2560], replicated, may hold values from 0.05 to 0.95
- receptance: bfloat16 [2560, 2560], P(None, 'head'), may hold values from -0.125 to 0.125
- key_weight: bfloat16 [2560, 2560], P(None, 'head'), may hold values from -0.125 to 0.125
- value_weight: bfloat16 [2560, 2560], P(None, 'head'), may hold values from -0.125 to 0.125
- decay_base: float32 [2560], P('head'), may hold values from -12.5 to -1.9
- decay_down_matrix: bfloat16 [2560, 96], replicated, may hold values from -0.125 to 0.125
- decay_up_matrix: bfloat16 [96, 2560], P(None, 'head'), may hold values from -0.625 to 0.625
- learn_base: float32 [2560], P('head'), may hold values from -1.5 to 1.5
- learning_down_matrix: bfloat16 [2560, 96], replicated, may hold values from -0.125 to 0.125
- learning_up_matrix: bfloat16 [96, 2560], P(None, 'head'), may hold values from -0.625 to 0.625
- key_scale: float32 [2560], P('head'), may hold values from 0.25 to 1.75
- key_blend: float32 [2560], P('head'), may hold values from 0.2 to 1
- norm_gain: float32 [2560], P('head'), may hold values from 0.25 to 1.75
- norm_bias: float32 [2560], P('head'), may hold values from -3 to 3
- output_weight: bfloat16 [2560, 2560], P('head'), may hold values from -0.125 to 0.125
Outputs:
- mixed_out: bfloat16 [2, 1024, 2560], P(None, 'seq', 'head')
The draws below stay inside these ranges and needn't reach their ends.
All inputs are finite; a program needn't handle non-finite values.
Results may differ from the reference program's by a relative error of at most 0.014.
Values may be sent and summed in bfloat16 or wider, within the bound.
A program may use at most 128 MiB of HBM per device.

```python
import math
import jax
import jax.numpy as jnp
from jax import lax

MODEL_WIDTH = 2560
LOW_RANK_WIDTH = 96
HEAD_SIZE = 64
SEQS = 2
LENGTH = 1024


def draw_decay_base(key, part):
    first, second = jax.random.split(jax.random.fold_in(key, 17))
    fast_share = 0.5
    fast = jax.random.bernoulli(first, fast_share, (MODEL_WIDTH,))
    spread = jax.random.uniform(second, (MODEL_WIDTH,), jnp.float32)
    fast_low = math.log(1.0 / 48.0)
    fast_high = math.log(1.0 / 12.0)
    slow_low = math.log(0.2 / LENGTH)
    slow_high = math.log(1.0 / LENGTH)
    rates = jnp.where(fast, fast_low + spread * (fast_high - fast_low), slow_low + spread * (slow_high - slow_low))
    return (rates + 0.5).astype(jnp.float32)


def level_of(stream_key, dims, shards, low, largest):
    def one(position, shards_of):
        draws = jax.random.uniform(jax.random.fold_in(jax.random.fold_in(stream_key, 6), position), (shards_of,), jnp.float32, low / len(shards), largest / len(shards))
        return jnp.repeat(jnp.exp(draws), dims[position] // shards_of).reshape((-1,) + (1,) * (len(dims) - position - 1))

    gain = one(*shards[0])
    for cut in shards[1:]:
        gain = gain * one(*cut)
    return gain


def bell_draw(rng, dims, scale, bound, shards=(), kind=jnp.bfloat16):
    level = level_of(rng, dims, shards, -0.22, 0.18) if shards else 1.0
    array = jax.random.normal(rng, dims, jnp.float32) * scale * level
    return jnp.minimum(jnp.maximum(array, -bound), bound).astype(kind)


def setup_inputs(seed: int = 0) -> dict:
    streams_of = jax.random.split(jax.random.key(seed), 17)
    return {
        "tokens": bell_draw(streams_of[0], (SEQS, LENGTH, MODEL_WIDTH), 1.0, 6.0, ((1, 8), (2, 4))),
        "token_mix": jnp.clip(jax.random.uniform(streams_of[1], (5, MODEL_WIDTH), jnp.float32, 0.05, 0.95), 0.05, 0.95),
        "receptance": bell_draw(streams_of[2], (MODEL_WIDTH, MODEL_WIDTH), MODEL_WIDTH ** -0.5, 0.125, ((1, 4),)),
        "key_weight": bell_draw(streams_of[3], (MODEL_WIDTH, MODEL_WIDTH), MODEL_WIDTH ** -0.5, 0.125, ((1, 4),)),
        "value_weight": bell_draw(streams_of[4], (MODEL_WIDTH, MODEL_WIDTH), MODEL_WIDTH ** -0.5, 0.125, ((1, 4),)),
        "decay_base": draw_decay_base(jax.random.fold_in(streams_of[16], 71), 0),
        "decay_down_matrix": bell_draw(streams_of[6], (MODEL_WIDTH, LOW_RANK_WIDTH), MODEL_WIDTH ** -0.5, 0.125),
        "decay_up_matrix": bell_draw(streams_of[7], (LOW_RANK_WIDTH, MODEL_WIDTH), LOW_RANK_WIDTH ** -0.5, 0.625, ((1, 4),)),
        "learn_base": jnp.clip(jax.random.uniform(streams_of[8], (MODEL_WIDTH,), jnp.float32, -1.5, 1.5) * level_of(streams_of[8], (MODEL_WIDTH,), ((0, 4),), -0.4, 0.0), -1.5, 1.5),
        "learning_down_matrix": bell_draw(streams_of[9], (MODEL_WIDTH, LOW_RANK_WIDTH), MODEL_WIDTH ** -0.5, 0.125),
        "learning_up_matrix": bell_draw(streams_of[10], (LOW_RANK_WIDTH, MODEL_WIDTH), LOW_RANK_WIDTH ** -0.5, 0.625, ((1, 4),)),
        "key_scale": jnp.clip(1.0 + 0.15 * jax.random.normal(streams_of[11], (MODEL_WIDTH,), jnp.float32), 0.25, 1.75),
        "key_blend": jnp.clip(0.2 + 0.8 * jax.random.uniform(streams_of[12], (MODEL_WIDTH,), jnp.float32) ** level_of(streams_of[12], (MODEL_WIDTH,), ((0, 4),), -0.2, 0.2), 0.2, 1.0),
        "norm_gain": jnp.clip(1.0 + 0.15 * jax.random.normal(streams_of[13], (MODEL_WIDTH,), jnp.float32), 0.25, 1.75),
        "norm_bias": bell_draw(streams_of[14], (MODEL_WIDTH,), 0.5, 3.0, ((0, 4),), jnp.float32),
        "output_weight": bell_draw(streams_of[15], (MODEL_WIDTH, MODEL_WIDTH), MODEL_WIDTH ** -0.5, 0.125, ((0, 4),)),
    }


def reference(tokens, token_mix, receptance, key_weight, value_weight, decay_base, decay_down_matrix, decay_up_matrix, learn_base, learning_down_matrix, learning_up_matrix, key_scale, key_blend, norm_gain, norm_bias, output_weight):
    seq_count, length, width = tokens.shape
    head_count = width // HEAD_SIZE
    row_count = seq_count * length
    current = tokens.astype(jnp.float32)
    earlier = jnp.concatenate([jnp.zeros((seq_count, 1, width), jnp.float32), current[:, :-1]], axis=1)
    change = earlier - current

    def blended(which):
        return (current + change * token_mix[which]).astype(jnp.bfloat16).reshape(row_count, width)

    def product(left, right):
        return jnp.dot(left, right, preferred_element_type=jnp.float32)
    recept_out = product(blended(0), receptance)
    key_raw = product(blended(2), key_weight)
    value_out = product(blended(3), value_weight)
    decay_hidden = jnp.tanh(product(blended(1), decay_down_matrix)).astype(jnp.bfloat16)
    learn_hidden = product(blended(4), learning_down_matrix).astype(jnp.bfloat16)
    decay_arg = decay_base + product(decay_hidden, decay_up_matrix)
    log_decay = -jnp.exp(-jax.nn.softplus(-decay_arg) - 0.5)
    learn_rate = jax.nn.sigmoid(learn_base + product(learn_hidden, learning_up_matrix))
    scaled = (key_raw * key_scale).reshape(row_count, head_count, HEAD_SIZE)
    unit_key = (scaled / jnp.sqrt(lax.optimization_barrier(jnp.sum(scaled * scaled, axis=-1, keepdims=True)) + 1e-06)).reshape(row_count, width)
    key_final = key_raw * (1.0 + (learn_rate - 1.0) * key_blend)

    def arrange(values):
        return values.reshape(seq_count, length, head_count, HEAD_SIZE).transpose(1, 0, 2, 3)

    def advance(state, item):
        recept_t, decay_t, unit_t, learn_t, key_t, value_t = item
        drained = jnp.einsum('shvk,shk->shv', state, -unit_t, precision=lax.Precision.HIGHEST)
        state = state * jnp.exp(decay_t)[:, :, None, :] + drained[..., None] * (unit_t * learn_t)[:, :, None, :] + value_t[..., None] * key_t[:, :, None, :]
        return (state, jnp.einsum('shvk,shk->shv', state, recept_t, precision=lax.Precision.HIGHEST))
    start = jnp.zeros((seq_count, head_count, HEAD_SIZE, HEAD_SIZE), jnp.float32)
    items = (arrange(recept_out), arrange(log_decay), arrange(unit_key), arrange(learn_rate), arrange(key_final), arrange(value_out))
    final_state, outputs = lax.scan(advance, start, items)
    wkv = outputs.transpose(1, 0, 2, 3).reshape(row_count, head_count, HEAD_SIZE)
    centred = wkv - lax.optimization_barrier(jnp.mean(wkv, axis=-1, keepdims=True))
    spread = lax.optimization_barrier(jnp.mean(centred * centred, axis=-1, keepdims=True))
    normed = (centred / jnp.sqrt(spread + 0.00064)).reshape(row_count, width) * norm_gain + norm_bias
    normed = normed.astype(jnp.bfloat16)
    result = product(normed, output_weight).astype(jnp.bfloat16)
    return result.reshape(seq_count, length, width)
```

```python
import functools
import math

import jax
import jax.numpy as jnp
from jax import lax
from jax.experimental import pallas as pl
from jax.experimental.pallas import tpu as pltpu
from jax.sharding import PartitionSpec as P

HEAD_SIZE = 64
PAIR = 2 * HEAD_SIZE
MESH = pl.DeviceIdType.MESH
F32 = jnp.float32
BF16 = jnp.bfloat16
DECAY_SCALE = math.exp(-0.5)


def dot(left, right):
    return jnp.dot(left, right, preferred_element_type=F32)


def dot_nt(left, right):
    return lax.dot_general(left, right, (((1,), (1,)), ((), ())), preferred_element_type=F32)


def dot_tn(left, right):
    return lax.dot_general(left, right, (((0,), (0,)), ((), ())), preferred_element_type=F32)


def iota(shape, axis):
    return lax.broadcasted_iota(jnp.int32, shape, axis)


def head_sum(values):
    first = iota(values.shape, 1) < HEAD_SIZE
    low = jnp.sum(jnp.where(first, values, 0.0), axis=-1, keepdims=True)
    high = jnp.sum(jnp.where(first, 0.0, values), axis=-1, keepdims=True)
    return jnp.where(first, low, high)


def diagonal(values):
    half = values.shape[1] // 2
    first = iota(values.shape, 1) < half
    zero = jnp.zeros_like(values)
    return jnp.concatenate(
        [jnp.where(first, values, zero), jnp.where(first, zero, values)], axis=0
    )


def chunk_maps(recept, key_raw, value, decay_arg, learn_arg, key_scale, key_blend):
    size = recept.shape[0]
    decay = -DECAY_SCALE / (1.0 + jnp.exp(-decay_arg))
    learn = 1.0 / (1.0 + jnp.exp(-learn_arg))
    scaled = key_raw * key_scale
    unit = scaled * lax.rsqrt(head_sum(scaled * scaled) + 1e-06)
    key = key_raw * (1.0 + (learn - 1.0) * key_blend)
    beta = unit * learn
    lower = (iota((size, size), 0) >= iota((size, size), 1)).astype(BF16)
    coarse = decay.astype(BF16)
    fine = (decay - coarse.astype(F32)).astype(BF16)
    sums = dot(lower, jnp.concatenate([coarse, fine], axis=1))
    cumul = sums[:, :PAIR] + sums[:, PAIR:]
    before = cumul - decay
    middle = cumul[size // 2 - 1 : size // 2, :]
    ending = cumul[size - 1 :, :]
    to_right = jnp.exp(middle - cumul)
    left = jnp.concatenate(
        [-unit * jnp.exp(before - middle), recept * jnp.exp(cumul - middle)], axis=0
    ).astype(BF16)
    with_beta = dot_nt(left, diagonal((beta * to_right).astype(BF16)))
    with_key = dot_nt(left, diagonal((key * to_right).astype(BF16)))
    row = iota((size, 2 * size), 0)
    column = iota((size, 2 * size), 1) % size
    strict = row > column
    within = row >= column
    lower_ab = jnp.where(strict, with_beta[:size], 0.0).astype(BF16)
    lower_ak = jnp.where(strict, with_key[:size], 0.0).astype(BF16)
    lower_rb = jnp.where(within, with_beta[size:], 0.0).astype(BF16)
    lower_rk = jnp.where(within, with_key[size:], 0.0).astype(BF16)
    zero = jnp.zeros_like(lower_ab)
    crossing = row ^ column
    inverse = jnp.where(row == column, 1.0, 0.0) + jnp.where(
        crossing == 1, lower_ab, zero
    ).astype(F32)
    block = 2
    while block < size:
        link = jnp.where((crossing >= block) & (crossing < 2 * block), lower_ab, zero)
        rounded = inverse.astype(BF16)
        half = dot(rounded, diagonal(link)).astype(BF16)
        inverse = inverse + dot(half, diagonal(rounded))
        block *= 2
    value_b = value.astype(BF16)
    from_value = dot(jnp.concatenate([lower_ak, lower_rk], axis=0), diagonal(value_b))
    alpha_exp = (-unit * jnp.exp(before)).astype(BF16)
    gains = dot(
        inverse.astype(BF16),
        jnp.concatenate(
            [diagonal(alpha_exp), diagonal(from_value[:size].astype(BF16))], axis=1
        ),
    )
    gains_b = gains.astype(BF16)
    answers = dot(
        lower_rb,
        jnp.concatenate([diagonal(gains_b[:, :PAIR]), diagonal(gains_b[:, PAIR:])], axis=1),
    )
    query = recept * jnp.exp(cumul) + answers[:, :PAIR]
    local = from_value[size:] + answers[:, PAIR:]
    to_end = jnp.exp(ending - cumul)
    ends = jnp.concatenate([beta * to_end, key * to_end], axis=0)
    sources = jnp.concatenate(
        [gains_b, jnp.concatenate([jnp.zeros_like(value_b), value_b], axis=1)], axis=0
    )
    total = dot(jnp.transpose(ends).astype(BF16), sources)
    same = iota((PAIR, PAIR), 0) == iota((PAIR, PAIR), 1)
    moving = total[:, :PAIR] + jnp.where(same, jnp.exp(ending), 0.0)
    adding = total[:, PAIR:]
    first = iota((HEAD_SIZE, PAIR), 1) < HEAD_SIZE
    map_low = jnp.where(first, moving[:HEAD_SIZE], pltpu.roll(adding[:HEAD_SIZE], HEAD_SIZE, 1))
    map_high = jnp.where(first, pltpu.roll(moving[HEAD_SIZE:], HEAD_SIZE, 1), adding[HEAD_SIZE:])
    return query, local, map_low, map_high


def group_norm(wkv, gain, bias):
    centred = wkv - head_sum(wkv) * (1.0 / HEAD_SIZE)
    spread = head_sum(centred * centred) * (1.0 / HEAD_SIZE)
    return centred * lax.rsqrt(spread + 0.00064) * gain + bias


def mix_kernel(
    seqs,
    axis,
    recept,
    key_raw,
    value,
    decay_hidden,
    learn_hidden,
    decay_up,
    learn_up,
    vectors,
    normed,
    query,
    local,
    maps,
    got,
    states,
    entry,
    map_send,
    map_recv,
    state_send,
    state_recv,
):
    n = lax.axis_size(axis)
    me = lax.axis_index(axis)
    rows, width = recept.shape
    size = rows // seqs
    heads = width // HEAD_SIZE
    slots = maps.shape[0]
    barrier = pltpu.get_barrier_semaphore()
    for d in range(1, n):
        pl.semaphore_signal(
            barrier, inc=1, device_id={axis: lax.rem(me + d, n)}, device_id_type=MESH
        )
    pl.semaphore_wait(barrier, n - 1)
    maps[...] = jnp.zeros_like(maps)

    def one(g, carry):
        lanes = pl.ds(pl.multiple_of(g * PAIR, PAIR), PAIR)
        for s in range(seqs):
            at = pl.ds(s * size, size)
            decay_arg = vectors[0:1, lanes] + dot(decay_hidden[at, :], decay_up[:, lanes])
            learn_arg = vectors[1:2, lanes] + dot(learn_hidden[at, :], learn_up[:, lanes])
            q, out, low, high = chunk_maps(
                recept[at, lanes],
                key_raw[at, lanes],
                value[at, lanes],
                decay_arg,
                learn_arg,
                vectors[2:3, lanes],
                vectors[3:4, lanes],
            )
            query[at, lanes] = q.astype(BF16)
            local[at, lanes] = out
            pair = s * heads + 2 * g
            maps[pair // n, pair % n] = low.astype(BF16)
            maps[(pair + 1) // n, (pair + 1) % n] = high.astype(BF16)
        return carry

    lax.fori_loop(0, width // PAIR, one, 0)

    def exchange(source, target, send, recv):
        copies = []
        for d in range(1, n):
            there = lax.rem(me + d, n)
            copy = pltpu.make_async_remote_copy(
                src_ref=source.at[:, there],
                dst_ref=target.at[:, me],
                send_sem=send.at[d],
                recv_sem=recv.at[d],
                device_id={axis: there},
                device_id_type=MESH,
            )
            copy.start()
            copies.append(copy)
        for slot in range(slots):
            target[slot, me] = source[slot, me]
        for copy in copies:
            copy.wait_recv()
        return copies

    sent_maps = exchange(maps, got, map_send, map_recv)
    pick = (iota((HEAD_SIZE, PAIR), 0) == iota((HEAD_SIZE, PAIR), 1)).astype(BF16)
    first = iota((HEAD_SIZE, PAIR), 1) < HEAD_SIZE
    packed = [jnp.zeros((HEAD_SIZE, PAIR), BF16)] * slots
    for i in range(n):
        for slot in range(slots):
            states[slot, i] = packed[slot]
        if i == n - 1:
            break
        for slot in range(slots):
            after = dot(got[slot, i], jnp.concatenate([packed[slot], pick], axis=0))
            whole = after + pltpu.roll(after, HEAD_SIZE, 1)
            coarse = whole.astype(BF16)
            fine = (whole - coarse.astype(F32)).astype(BF16)
            packed[slot] = jnp.where(first, coarse, fine)
    sent_states = exchange(states, entry, state_send, state_recv)

    def finish(g, carry):
        lanes = pl.ds(pl.multiple_of(g * PAIR, PAIR), PAIR)
        for s in range(seqs):
            at = pl.ds(s * size, size)
            pair = s * heads + 2 * g
            low = entry[pair // n, pair % n]
            high = entry[(pair + 1) // n, (pair + 1) % n]
            zero = jnp.zeros_like(low)
            both = jnp.concatenate(
                [
                    jnp.where(first, low, zero),
                    jnp.where(first, zero, jnp.concatenate([zero[:, :HEAD_SIZE], high[:, :HEAD_SIZE]], axis=1)),
                ],
                axis=0,
            )
            wkv = local[at, lanes] + dot(query[at, lanes], both)
            normed[at, lanes] = group_norm(
                wkv, vectors[4:5, lanes], vectors[5:6, lanes]
            ).astype(BF16)
        return carry

    lax.fori_loop(0, width // PAIR, finish, 0)
    for copy in sent_maps + sent_states:
        copy.wait_send()


def out_kernel(
    axis, normed, weight, out, part, mate_got, across, across_got, mate_send, mate_recv, send, recv
):
    n = lax.axis_size(axis)
    me = lax.axis_index(axis)
    chips = n // 2
    chip, core = me // 2, me % 2
    mate = chip * 2 + (1 - core)
    width = out.shape[1]
    barrier = pltpu.get_barrier_semaphore()
    peers = [mate] + [lax.rem(chip + d, chips) * 2 + core for d in range(1, chips)]
    for peer in peers:
        pl.semaphore_signal(barrier, inc=1, device_id={axis: peer}, device_id_type=MESH)
    pl.semaphore_wait(barrier, chips)

    def columns(index):
        if len(weight.shape) == 3:
            return weight[index]
        return weight[:, pl.ds(pl.multiple_of(index * width, width), width)]

    to_mate = []
    order = list(range(1, chips)) + [0]
    for d in order:
        other = lax.rem(chip + d, chips)
        part[d] = dot(normed[...], columns(other * 2 + 1 - core)).astype(BF16)
        copy = pltpu.make_async_remote_copy(
            src_ref=part.at[d],
            dst_ref=mate_got.at[d],
            send_sem=mate_send.at[d],
            recv_sem=mate_recv.at[d],
            device_id={axis: mate},
            device_id_type=MESH,
        )
        copy.start()
        to_mate.append(copy)
    moving = []
    for step, d in enumerate(order):
        other = lax.rem(chip + d, chips)
        mine = dot(normed[...], columns(other * 2 + core))
        to_mate[step].wait_recv()
        mine = mine + mate_got[d].astype(F32)
        if d == 0:
            break
        across[d] = mine.astype(BF16)
        copy = pltpu.make_async_remote_copy(
            src_ref=across.at[d],
            dst_ref=across_got.at[d],
            send_sem=send.at[d],
            recv_sem=recv.at[d],
            device_id={axis: other * 2 + core},
            device_id_type=MESH,
        )
        copy.start()
        moving.append(copy)
    for step, copy in enumerate(moving):
        copy.wait_recv()
        mine = mine + across_got[step + 1].astype(F32)
    out[...] = mine.astype(BF16)
    for copy in to_mate + moving:
        copy.wait_send()


def vmem():
    return pl.BlockSpec(memory_space=pltpu.VMEM)


def mix(operands, seqs, axis):
    rows, width = operands[0].shape
    n = lax.axis_size(axis)
    pairs = seqs * width // HEAD_SIZE
    slots = -(-pairs // n)
    table = pltpu.VMEM((slots, n, HEAD_SIZE, PAIR), BF16)
    sems = pltpu.SemaphoreType.DMA((n,))
    return pl.pallas_call(
        functools.partial(mix_kernel, seqs, axis),
        out_shape=jax.ShapeDtypeStruct((rows, width), BF16),
        in_specs=[vmem()] * len(operands),
        out_specs=vmem(),
        scratch_shapes=[
            pltpu.VMEM((rows, width), BF16),
            pltpu.VMEM((rows, width), F32),
            table,
            table,
            table,
            table,
            sems,
            sems,
            sems,
            sems,
        ],
        compiler_params=pltpu.CompilerParams(
            collective_id=0, has_side_effects=True, vmem_limit_bytes=48 * 2**20
        ),
    )(*operands)


def project_out(normed, weight, out_width, axis):
    rows = normed.shape[0]
    chips = lax.axis_size(axis) // 2
    table = pltpu.VMEM((chips, rows, out_width), BF16)
    sems = pltpu.SemaphoreType.DMA((chips,))
    return pl.pallas_call(
        functools.partial(out_kernel, axis),
        out_shape=jax.ShapeDtypeStruct((rows, out_width), BF16),
        in_specs=[vmem()] * 2,
        out_specs=vmem(),
        scratch_shapes=[table, table, table, table, sems, sems, sems, sems],
        compiler_params=pltpu.CompilerParams(
            collective_id=1, has_side_effects=True, vmem_limit_bytes=48 * 2**20
        ),
    )(normed, weight)


def body(
    tokens,
    token_mix,
    receptance,
    key_weight,
    value_weight,
    decay_base,
    decay_down_matrix,
    decay_up_matrix,
    learn_base,
    learning_down_matrix,
    learning_up_matrix,
    key_scale,
    key_blend,
    norm_gain,
    norm_bias,
    output_weight,
):
    seqs, length, own_width = tokens.shape
    rows = seqs * length
    lack = -own_width % PAIR
    if lack:
        wider = lambda array: jnp.pad(array, [(0, 0)] * (array.ndim - 1) + [(0, lack)])
        receptance, key_weight, value_weight, decay_up_matrix, learning_up_matrix = map(
            wider, (receptance, key_weight, value_weight, decay_up_matrix, learning_up_matrix)
        )
        decay_base, learn_base, key_scale, key_blend, norm_gain, norm_bias = map(
            wider, (decay_base, learn_base, key_scale, key_blend, norm_gain, norm_bias)
        )
        output_weight = jnp.pad(output_weight, [(0, lack), (0, 0)])
        output_weight = output_weight.reshape(own_width + lack, -1, own_width).transpose(1, 0, 2)
    seq_devices = lax.axis_size("seq")
    boundary = lax.ppermute(
        tokens[:, length - 1 :, :], "seq", [(i, i + 1) for i in range(seq_devices - 1)]
    )
    wide = lax.all_gather(
        jnp.concatenate([boundary, tokens], axis=1), "head", axis=2, tiled=True
    )
    current = wide[:, 1:].astype(F32)
    change = wide[:, :-1].astype(F32) - current
    extent = wide.shape[2]

    def project(which, weight):
        blended = (current + change * token_mix[which]).astype(BF16).reshape(rows, extent)
        return dot(blended, weight)

    decay_hidden = jnp.tanh(project(1, decay_down_matrix)).astype(BF16)
    learn_hidden = project(4, learning_down_matrix).astype(BF16)
    vectors = jnp.stack([decay_base, learn_base, key_scale, key_blend, norm_gain, norm_bias])
    operands = (
        project(0, receptance),
        project(2, key_weight),
        project(3, value_weight),
        decay_hidden,
        learn_hidden,
        decay_up_matrix,
        learning_up_matrix,
        vectors,
    )
    normed = mix(operands, seqs, "seq")
    result = project_out(normed, output_weight, own_width, "head")
    return result.reshape(seqs, length, own_width)


def solution(mesh):
    placed = (
        P(None, "seq", "head"),
        P(),
        P(None, "head"),
        P(None, "head"),
        P(None, "head"),
        P("head"),
        P(),
        P(None, "head"),
        P("head"),
        P(),
        P(None, "head"),
        P("head"),
        P("head"),
        P("head"),
        P("head"),
        P("head", None),
    )
    return jax.shard_map(
        body, mesh=mesh, in_specs=placed, out_specs=P(None, "seq", "head"), check_vma=False
    )
```

```python
import math

import jax
import jax.numpy as jnp
from jax import lax
from jax.experimental import pallas as pl
from jax.experimental.pallas import tpu as pltpu
from jax.sharding import PartitionSpec as P

HEAD_SIZE = 64
PAIR = 2 * HEAD_SIZE
MESH = pl.DeviceIdType.MESH
F32 = jnp.float32
BF16 = jnp.bfloat16
DECAY_SCALE = math.exp(-0.5)


def dot(left, right):
    return jnp.dot(left, right, preferred_element_type=F32)


def dot_nt(left, right):
    return lax.dot_general(left, right, (((1,), (1,)), ((), ())), preferred_element_type=F32)


def dot_tn(left, right):
    return lax.dot_general(left, right, (((0,), (0,)), ((), ())), preferred_element_type=F32)


def iota(shape, axis):
    return lax.broadcasted_iota(jnp.int32, shape, axis)


def head_sum(values):
    first = iota(values.shape, 1) < HEAD_SIZE
    low = jnp.sum(jnp.where(first, values, 0.0), axis=-1, keepdims=True)
    high = jnp.sum(jnp.where(first, 0.0, values), axis=-1, keepdims=True)
    return jnp.where(first, low, high)


def diagonal(values):
    half = values.shape[1] // 2
    first = iota(values.shape, 1) < half
    zero = jnp.zeros_like(values)
    return jnp.concatenate(
        [jnp.where(first, values, zero), jnp.where(first, zero, values)], axis=0
    )


def interleaved(units):
    while True:
        results = [next(unit) for unit in units]
        if results[0] is not None:
            return results


def chunk_maps(recept, key_raw, value, decay_arg, learn_arg, key_scale, key_blend):
    size = recept.shape[0]
    decay = -DECAY_SCALE / (1.0 + jnp.exp(-decay_arg))
    learn = 1.0 / (1.0 + jnp.exp(-learn_arg))
    scaled = key_raw * key_scale
    unit = scaled * lax.rsqrt(head_sum(scaled * scaled) + 1e-06)
    key = key_raw * (1.0 + (learn - 1.0) * key_blend)
    beta = unit * learn
    lower = (iota((size, size), 0) >= iota((size, size), 1)).astype(BF16)
    coarse = decay.astype(BF16)
    fine = (decay - coarse.astype(F32)).astype(BF16)
    sums = dot(lower, jnp.concatenate([coarse, fine], axis=1))
    yield
    cumul = sums[:, :PAIR] + sums[:, PAIR:]
    before = cumul - decay
    middle = cumul[size // 2 - 1 : size // 2, :]
    ending = cumul[size - 1 :, :]
    to_right = jnp.exp(middle - cumul)
    left = jnp.concatenate(
        [-unit * jnp.exp(before - middle), recept * jnp.exp(cumul - middle)], axis=0
    ).astype(BF16)
    with_beta = dot_nt(left, diagonal((beta * to_right).astype(BF16)))
    with_key = dot_nt(left, diagonal((key * to_right).astype(BF16)))
    yield
    row = iota((size, 2 * size), 0)
    column = iota((size, 2 * size), 1) % size
    strict = row > column
    within = row >= column
    lower_ab = jnp.where(strict, with_beta[:size], 0.0).astype(BF16)
    lower_ak = jnp.where(strict, with_key[:size], 0.0).astype(BF16)
    lower_rb = jnp.where(within, with_beta[size:], 0.0).astype(BF16)
    lower_rk = jnp.where(within, with_key[size:], 0.0).astype(BF16)
    zero = jnp.zeros_like(lower_ab)
    crossing = row ^ column
    inverse = jnp.where(row == column, 1.0, 0.0) + jnp.where(
        crossing == 1, lower_ab, zero
    ).astype(F32)
    block = 2
    while block < size:
        link = jnp.where((crossing >= block) & (crossing < 2 * block), lower_ab, zero)
        rounded = inverse.astype(BF16)
        half = dot(rounded, diagonal(link)).astype(BF16)
        yield
        inverse = inverse + dot(half, diagonal(rounded))
        yield
        block *= 2
    yield
    value_b = value.astype(BF16)
    from_value = dot(jnp.concatenate([lower_ak, lower_rk], axis=0), diagonal(value_b))
    yield
    alpha_exp = (-unit * jnp.exp(before)).astype(BF16)
    gains = dot(
        inverse.astype(BF16),
        jnp.concatenate(
            [diagonal(alpha_exp), diagonal(from_value[:size].astype(BF16))], axis=1
        ),
    )
    yield
    gains_b = gains.astype(BF16)
    answers = dot(
        lower_rb,
        jnp.concatenate([diagonal(gains_b[:, :PAIR]), diagonal(gains_b[:, PAIR:])], axis=1),
    )
    yield
    query = recept * jnp.exp(cumul) + answers[:, :PAIR]
    local = from_value[size:] + answers[:, PAIR:]
    to_end = jnp.exp(ending - cumul)
    ends = jnp.concatenate([beta * to_end, key * to_end], axis=0)
    sources = jnp.concatenate(
        [gains_b, jnp.concatenate([jnp.zeros_like(value_b), value_b], axis=1)], axis=0
    )
    total = dot(jnp.transpose(ends).astype(BF16), sources)
    yield
    same = iota((PAIR, PAIR), 0) == iota((PAIR, PAIR), 1)
    moving = total[:, :PAIR] + jnp.where(same, jnp.exp(ending), 0.0)
    adding = total[:, PAIR:]
    first = iota((HEAD_SIZE, PAIR), 1) < HEAD_SIZE
    map_low = jnp.where(first, moving[:HEAD_SIZE], pltpu.roll(adding[:HEAD_SIZE], HEAD_SIZE, 1))
    map_high = jnp.where(first, pltpu.roll(moving[HEAD_SIZE:], HEAD_SIZE, 1), adding[HEAD_SIZE:])
    yield query, local, map_low, map_high


def group_norm(wkv, gain, bias):
    centred = wkv - head_sum(wkv) * (1.0 / HEAD_SIZE)
    spread = head_sum(centred * centred) * (1.0 / HEAD_SIZE)
    return centred * lax.rsqrt(spread + 0.00064) * gain + bias


class Remote:
    def __init__(self):
        self.started = []

    def send(self, source, target, send, recv, device):
        copy = pltpu.make_async_remote_copy(
            src_ref=source,
            dst_ref=target,
            send_sem=send,
            recv_sem=recv,
            device_id=device,
            device_id_type=MESH,
        )
        copy.start()
        self.started.append(copy)
        return copy

    def drain(self):
        for copy in self.started:
            copy.wait_send()


def layer_kernel(
    tokens_hbm,
    token_mix,
    weights_hbm,
    downs_hbm,
    ups,
    vectors,
    output_hbm,
    out,
    wide,
    edge,
    weights,
    downs,
    output_weight,
    sums,
    low_sums,
    query,
    local,
    normed,
    maps,
    got,
    states,
    entry,
    part,
    mate_got,
    across,
    across_got,
    load_sem,
    own_sem,
    gather_send,
    gather_recv,
    pass_send,
    pass_recv,
    edge_send,
    edge_recv,
    map_send,
    map_recv,
    state_send,
    state_recv,
    mate_send,
    mate_recv,
    across_send,
    across_recv,
):
    n = lax.axis_size("seq")
    me = lax.axis_index("seq")
    peers = lax.axis_size("head")
    place = lax.axis_index("head")
    chips = peers // 2
    chip, core = place // 2, place % 2
    mate = chip * 2 + 1 - core
    _, seqs, size, own = wide.shape
    width = local.shape[1]
    heads = width // HEAD_SIZE
    slots = maps.shape[0]
    edge_rows = edge.shape[2]
    remote = Remote()

    def at(seq, head):
        return {"seq": seq, "head": head}

    loads = []
    sources = list(weights_hbm) + list(downs_hbm) + [output_hbm]
    targets = list(weights) + list(downs) + [output_weight]
    own_copy = pltpu.make_async_copy(tokens_hbm, wide.at[place], own_sem.at[0])
    own_copy.start()
    for i, (source, target) in enumerate(zip(sources, targets)):
        copy = pltpu.make_async_copy(source, target, load_sem.at[i])
        copy.start()
        loads.append(copy)

    barrier = pltpu.get_barrier_semaphore()

    def greet(seq, head):
        pl.semaphore_signal(barrier, inc=1, device_id=at(seq, head), device_id_type=MESH)

    before, after = lax.rem(me + n - 1, n), lax.rem(me + 1, n)
    for d in range(1, n):
        greet(lax.rem(me + d, n), place)
    greet(me, mate)
    for d in range(1, chips):
        greet(me, lax.rem(chip + d, chips) * 2 + core)
    for d in range(1, peers):
        greet(before, lax.rem(place + d, peers))
    pl.semaphore_wait(barrier, n - 1 + chips + peers - 1)

    from_across = []
    for s in range(seqs):
        for d in range(1, chips):
            copy = remote.send(
                tokens_hbm.at[s],
                wide.at[place, s],
                gather_send.at[d, s],
                gather_recv.at[d, s],
                at(me, lax.rem(chip + d, chips) * 2 + core),
            )
            from_across.append((s, d, copy))
    from_mate = []
    for s in range(seqs):
        from_mate.append(
            remote.send(
                tokens_hbm.at[s],
                wide.at[place, s],
                gather_send.at[0, s],
                gather_recv.at[0, s],
                at(me, mate),
            )
        )
    edges = []
    for d in range(peers):
        edges.append(
            remote.send(
                tokens_hbm.at[:, pl.ds(size - edge_rows, edge_rows), :],
                edge.at[place],
                edge_send.at[d],
                edge_recv.at[d],
                at(after, lax.rem(place + d, peers)),
            )
        )
    maps[...] = jnp.zeros_like(maps)
    started = (me > 0).astype(F32)

    def absorb(h, initial):
        if len(token_mix.shape) == 3:
            mixing = token_mix[h]
        else:
            mixing = token_mix[:, pl.ds(pl.multiple_of(h * own, own), own)]
        currents, changes = [], []
        for s in range(seqs):
            current = wide[h, s].astype(F32)
            row = edge[h, s].astype(F32)[edge_rows - 1 :, :] * started
            earlier = jnp.where(iota(current.shape, 0) == 0, row, pltpu.roll(current, 1, 0))
            currents.append(current)
            changes.append(earlier - current)
        current = jnp.concatenate(currents, axis=0)
        change = jnp.concatenate(changes, axis=0)
        rows = pl.ds(pl.multiple_of(h * own, own), own)
        for j, total, weight in (
            (0, sums[0], weights[0]),
            (2, sums[1], weights[1]),
            (3, sums[2], weights[2]),
            (1, low_sums[0], downs[0]),
            (4, low_sums[1], downs[1]),
        ):
            blended = (current + change * mixing[j : j + 1, :]).astype(BF16)
            term = dot(blended, weight[rows, :])
            total[...] = term if initial else total[...] + term

    own_copy.wait()
    for copy in edges:
        copy.wait_recv()
    for copy in loads[:-1]:
        copy.wait()
    absorb(place, True)
    for copy in from_mate:
        copy.wait_recv()
    absorb(mate, False)
    passed = []
    for s, d, copy in from_across:
        copy.wait_recv()
        came = lax.rem(chip + chips - d, chips) * 2 + core
        passed.append(
            remote.send(
                wide.at[came, s],
                wide.at[came, s],
                pass_send.at[d, s],
                pass_recv.at[d, s],
                at(me, mate),
            )
        )
    for d in range(1, chips):
        absorb(lax.rem(chip + chips - d, chips) * 2 + core, False)
    for copy in passed:
        copy.wait_recv()
    for d in range(1, chips):
        absorb(lax.rem(chip + chips - d, chips) * 2 + 1 - core, False)

    def one(s, carry):
        at_rows = pl.ds(pl.multiple_of(s * size, size), size)
        decay_hidden = jnp.tanh(low_sums[0][at_rows, :]).astype(BF16)
        learn_hidden = low_sums[1][at_rows, :].astype(BF16)
        units = []
        for g in range(width // PAIR):
            lanes = pl.ds(g * PAIR, PAIR)
            units.append(
                chunk_maps(
                    sums[0][at_rows, lanes],
                    sums[1][at_rows, lanes],
                    sums[2][at_rows, lanes],
                    vectors[0][:, lanes] + dot(decay_hidden, ups[0][:, lanes]),
                    vectors[1][:, lanes] + dot(learn_hidden, ups[1][:, lanes]),
                    vectors[2][:, lanes],
                    vectors[3][:, lanes],
                )
            )
        for g, (q, rest, low, high) in enumerate(interleaved(units)):
            lanes = pl.ds(g * PAIR, PAIR)
            query[at_rows, lanes] = q.astype(BF16)
            local[at_rows, lanes] = rest
            pair = s * heads + 2 * g
            maps[pair // n, pair % n] = low.astype(BF16)
            maps[(pair + 1) // n, (pair + 1) % n] = high.astype(BF16)
        return carry

    lax.fori_loop(0, seqs, one, 0)

    def exchange(source, target, send, recv):
        copies = []
        for d in range(1, n):
            there = lax.rem(me + d, n)
            copies.append(
                remote.send(
                    source.at[:, there],
                    target.at[:, me],
                    send.at[d],
                    recv.at[d],
                    at(there, place),
                )
            )
        for slot in range(slots):
            target[slot, me] = source[slot, me]
        for copy in copies:
            copy.wait_recv()

    exchange(maps, got, map_send, map_recv)
    pick = (iota((HEAD_SIZE, PAIR), 0) == iota((HEAD_SIZE, PAIR), 1)).astype(BF16)
    first = iota((HEAD_SIZE, PAIR), 1) < HEAD_SIZE
    packed = [jnp.zeros((HEAD_SIZE, PAIR), BF16)] * slots
    for i in range(n):
        for slot in range(slots):
            states[slot, i] = packed[slot]
        if i == n - 1:
            break
        for slot in range(slots):
            follow = dot(got[slot, i], jnp.concatenate([packed[slot], pick], axis=0))
            whole = follow + pltpu.roll(follow, HEAD_SIZE, 1)
            coarse = whole.astype(BF16)
            fine = (whole - coarse.astype(F32)).astype(BF16)
            packed[slot] = jnp.where(first, coarse, fine)
    exchange(states, entry, state_send, state_recv)

    def finish(s):
        at_rows = pl.ds(s * size, size)
        for g in range(width // PAIR):
            lanes = pl.ds(g * PAIR, PAIR)
            pair = s * heads + 2 * g
            low = entry[pair // n, pair % n]
            high = entry[(pair + 1) // n, (pair + 1) % n]
            zero = jnp.zeros_like(low)
            shifted = jnp.concatenate([zero[:, :HEAD_SIZE], high[:, :HEAD_SIZE]], axis=1)
            both = jnp.concatenate([jnp.where(first, low, zero), shifted], axis=0)
            wkv = local[at_rows, lanes] + dot(query[at_rows, lanes], both)
            normed[at_rows, lanes] = group_norm(
                wkv, vectors[4][:, lanes], vectors[5][:, lanes]
            ).astype(BF16)

    def columns(index):
        if len(output_weight.shape) == 3:
            return output_weight[index]
        return output_weight[:, pl.ds(pl.multiple_of(index * own, own), own)]

    loads[-1].wait()
    order = list(range(1, chips)) + [0]
    to_mate = {}
    for s in range(seqs):
        finish(s)
        at_rows = pl.ds(s * size, size)
        for d in order:
            other = lax.rem(chip + d, chips)
            part[d, s] = dot(normed[at_rows, :], columns(other * 2 + 1 - core)).astype(BF16)
            to_mate[d, s] = remote.send(
                part.at[d, s],
                mate_got.at[d, s],
                mate_send.at[d, s],
                mate_recv.at[d, s],
                at(me, mate),
            )
        for d in order[:-1]:
            other = lax.rem(chip + d, chips)
            mine = dot(normed[at_rows, :], columns(other * 2 + core))
            to_mate[d, s].wait_recv()
            across[d, s] = (mine + mate_got[d, s].astype(F32)).astype(BF16)
            to_mate[d, s, "far"] = remote.send(
                across.at[d, s],
                across_got.at[d, s],
                across_send.at[d, s],
                across_recv.at[d, s],
                at(me, other * 2 + core),
            )
    for s in range(seqs):
        at_rows = pl.ds(s * size, size)
        mine = dot(normed[at_rows, :], columns(place))
        to_mate[0, s].wait_recv()
        mine = mine + mate_got[0, s].astype(F32)
        for d in order[:-1]:
            to_mate[d, s, "far"].wait_recv()
            mine = mine + across_got[d, s].astype(F32)
        out[at_rows, :] = mine.astype(BF16)
    remote.drain()


def layer(tokens, token_mix, weights, downs, ups, vectors, output_weight):
    seqs, size, own = tokens.shape
    rows, width = seqs * size, weights[0].shape[1]
    n, peers = lax.axis_size("seq"), lax.axis_size("head")
    chips = peers // 2
    slots = -(-(seqs * width // HEAD_SIZE) // n)
    edge_rows = min(16, size)
    sems = pltpu.SemaphoreType.DMA
    table = pltpu.VMEM((slots, n, HEAD_SIZE, PAIR), BF16)
    piece = pltpu.VMEM((chips, seqs, size, own), BF16)
    inside = pl.BlockSpec(memory_space=pltpu.VMEM)
    outside = pl.BlockSpec(memory_space=pl.ANY)

    def like(array):
        return pltpu.VMEM(array.shape, array.dtype)

    return pl.pallas_call(
        layer_kernel,
        out_shape=jax.ShapeDtypeStruct((rows, own), BF16),
        in_specs=[outside, inside, [outside] * 3, [outside] * 2, [inside] * 2, [inside] * 6, outside],
        out_specs=inside,
        scratch_shapes=[
            pltpu.VMEM((peers, seqs, size, own), BF16),
            pltpu.VMEM((peers, seqs, edge_rows, own), BF16),
            [like(weight) for weight in weights],
            [like(down) for down in downs],
            like(output_weight),
            [pltpu.VMEM((rows, width), F32)] * 3,
            [pltpu.VMEM((rows, down.shape[1]), F32) for down in downs],
            pltpu.VMEM((rows, width), BF16),
            pltpu.VMEM((rows, width), F32),
            pltpu.VMEM((rows, width), BF16),
            table,
            table,
            table,
            table,
            piece,
            piece,
            piece,
            piece,
            sems((len(weights) + len(downs) + 1,)),
            sems((1,)),
            sems((chips, seqs)),
            sems((chips, seqs)),
            sems((chips, seqs)),
            sems((chips, seqs)),
            sems((peers,)),
            sems((peers,)),
            sems((n,)),
            sems((n,)),
            sems((n,)),
            sems((n,)),
            sems((chips, seqs)),
            sems((chips, seqs)),
            sems((chips, seqs)),
            sems((chips, seqs)),
        ],
        compiler_params=pltpu.CompilerParams(
            collective_id=0, has_side_effects=True, vmem_limit_bytes=56 * 2**20
        ),
    )(tokens, token_mix, weights, downs, ups, vectors, output_weight)


def body(
    tokens,
    token_mix,
    receptance,
    key_weight,
    value_weight,
    decay_base,
    decay_down_matrix,
    decay_up_matrix,
    learn_base,
    learning_down_matrix,
    learning_up_matrix,
    key_scale,
    key_blend,
    norm_gain,
    norm_bias,
    output_weight,
):
    seqs, length, own_width = tokens.shape
    lack = -own_width % PAIR
    if lack:
        wider = lambda array: jnp.pad(array, [(0, 0)] * (array.ndim - 1) + [(0, lack)])
        receptance, key_weight, value_weight, decay_up_matrix, learning_up_matrix = map(
            wider, (receptance, key_weight, value_weight, decay_up_matrix, learning_up_matrix)
        )
        decay_base, learn_base, key_scale, key_blend, norm_gain, norm_bias = map(
            wider, (decay_base, learn_base, key_scale, key_blend, norm_gain, norm_bias)
        )
        output_weight = jnp.pad(output_weight, [(0, lack), (0, 0)])
        output_weight = output_weight.reshape(own_width + lack, -1, own_width).transpose(1, 0, 2)
        token_mix = token_mix.reshape(token_mix.shape[0], -1, own_width).transpose(1, 0, 2)
    vectors = [decay_base, learn_base, key_scale, key_blend, norm_gain, norm_bias]
    result = layer(
        tokens,
        token_mix,
        [receptance, key_weight, value_weight],
        [decay_down_matrix, learning_down_matrix],
        [decay_up_matrix, learning_up_matrix],
        [vector[None] for vector in vectors],
        output_weight,
    )
    return result.reshape(seqs, length, own_width)


def solution(mesh):
    placed = (
        P(None, "seq", "head"),
        P(),
        P(None, "head"),
        P(None, "head"),
        P(None, "head"),
        P("head"),
        P(),
        P(None, "head"),
        P("head"),
        P(),
        P(None, "head"),
        P("head"),
        P("head"),
        P("head"),
        P("head"),
        P("head", None),
    )
    return jax.shard_map(
        body, mesh=mesh, in_specs=placed, out_specs=P(None, "seq", "head"), check_vma=False
    )
```

```python
import math

import jax
import jax.numpy as jnp
from jax import lax
from jax.experimental import pallas as pl
from jax.experimental.pallas import tpu as pltpu
from jax.sharding import PartitionSpec as P

HEAD_SIZE = 64
PAIR = 2 * HEAD_SIZE
MESH = pl.DeviceIdType.MESH
F32 = jnp.float32
BF16 = jnp.bfloat16
DECAY_SCALE = math.exp(-0.5)


def dot(left, right):
    return jnp.dot(left, right, preferred_element_type=F32)


def dot_nt(left, right):
    return lax.dot_general(left, right, (((1,), (1,)), ((), ())), preferred_element_type=F32)


def dot_tn(left, right):
    return lax.dot_general(left, right, (((0,), (0,)), ((), ())), preferred_element_type=F32)


def iota(shape, axis):
    return lax.broadcasted_iota(jnp.int32, shape, axis)


def head_sum(values):
    first = iota(values.shape, 1) < HEAD_SIZE
    low = jnp.sum(jnp.where(first, values, 0.0), axis=-1, keepdims=True)
    high = jnp.sum(jnp.where(first, 0.0, values), axis=-1, keepdims=True)
    return jnp.where(first, low, high)


def diagonal(values):
    half = values.shape[1] // 2
    if half % PAIR == 0:
        zero = jnp.zeros_like(values[:, :half])
        upper = jnp.concatenate([values[:, :half], zero], axis=1)
        return jnp.concatenate(
            [upper, jnp.concatenate([zero, values[:, half:]], axis=1)], axis=0
        )
    first = iota(values.shape, 1) < half
    zero = jnp.zeros_like(values)
    return jnp.concatenate(
        [jnp.where(first, values, zero), jnp.where(first, zero, values)], axis=0
    )


def interleaved(units):
    while True:
        results = [next(unit) for unit in units]
        if results[0] is not None:
            return results


def link_masks(size):
    crossing = iota((size, 2 * size), 0) ^ (iota((size, 2 * size), 1) % size)
    blocks = [2**level for level in range((size - 1).bit_length())]
    return [((crossing >= b) & (crossing < 2 * b)).astype(F32).astype(BF16) for b in blocks]


def chunk_maps(masks, recept, key_raw, value, decay_arg, learn_arg, key_scale, key_blend):
    size = recept.shape[0]
    decay = -DECAY_SCALE / (1.0 + jnp.exp(-decay_arg))
    learn = 1.0 / (1.0 + jnp.exp(-learn_arg))
    scaled = key_raw * key_scale
    unit = scaled * lax.rsqrt(head_sum(scaled * scaled) + 1e-06)
    key = key_raw * (1.0 + (learn - 1.0) * key_blend)
    beta = unit * learn
    lower = (iota((size, size), 0) >= iota((size, size), 1)).astype(BF16)
    coarse = decay.astype(BF16)
    fine = (decay - coarse.astype(F32)).astype(BF16)
    sums = dot(lower, jnp.concatenate([coarse, fine], axis=1))
    yield
    cumul = sums[:, :PAIR] + sums[:, PAIR:]
    before = cumul - decay
    middle = cumul[size // 2 - 1 : size // 2, :]
    ending = cumul[size - 1 :, :]
    to_right = jnp.exp(middle - cumul)
    left = jnp.concatenate(
        [-unit * jnp.exp(before - middle), recept * jnp.exp(cumul - middle)], axis=0
    ).astype(BF16)
    with_beta = dot_nt(left, diagonal((beta * to_right).astype(BF16)))
    with_key = dot_nt(left, diagonal((key * to_right).astype(BF16)))
    yield
    row = iota((size, 2 * size), 0)
    column = iota((size, 2 * size), 1) % size
    strict = row > column
    within = row >= column
    lower_ab = jnp.where(strict, with_beta[:size], 0.0).astype(BF16)
    lower_ak = jnp.where(strict, with_key[:size], 0.0).astype(BF16)
    lower_rb = jnp.where(within, with_beta[size:], 0.0).astype(BF16)
    lower_rk = jnp.where(within, with_key[size:], 0.0).astype(BF16)
    inverse = jnp.where(row == column, 1.0, 0.0) + (lower_ab * masks[0]).astype(F32)
    for mask in masks[1:]:
        link = lower_ab * mask
        rounded = inverse.astype(BF16)
        half = dot(rounded, diagonal(link)).astype(BF16)
        yield
        inverse = inverse + dot(half, diagonal(rounded))
        yield
    yield
    value_b = value.astype(BF16)
    from_value = dot(jnp.concatenate([lower_ak, lower_rk], axis=0), diagonal(value_b))
    yield
    alpha_exp = (-unit * jnp.exp(before)).astype(BF16)
    gains = dot(
        inverse.astype(BF16),
        jnp.concatenate(
            [diagonal(alpha_exp), diagonal(from_value[:size].astype(BF16))], axis=1
        ),
    )
    yield
    gains_b = gains.astype(BF16)
    answers = dot(
        lower_rb,
        jnp.concatenate([diagonal(gains_b[:, :PAIR]), diagonal(gains_b[:, PAIR:])], axis=1),
    )
    yield
    query = recept * jnp.exp(cumul) + answers[:, :PAIR]
    local = from_value[size:] + answers[:, PAIR:]
    to_end = jnp.exp(ending - cumul)
    ends = jnp.concatenate([beta * to_end, key * to_end], axis=0)
    sources = jnp.concatenate(
        [gains_b, jnp.concatenate([jnp.zeros_like(value_b), value_b], axis=1)], axis=0
    )
    total = dot(jnp.transpose(ends).astype(BF16), sources)
    yield
    same = iota((PAIR, PAIR), 0) == iota((PAIR, PAIR), 1)
    moving = total[:, :PAIR] + jnp.where(same, jnp.exp(ending), 0.0)
    adding = total[:, PAIR:]
    first = iota((HEAD_SIZE, PAIR), 1) < HEAD_SIZE
    map_low = jnp.where(first, moving[:HEAD_SIZE], pltpu.roll(adding[:HEAD_SIZE], HEAD_SIZE, 1))
    map_high = jnp.where(first, pltpu.roll(moving[HEAD_SIZE:], HEAD_SIZE, 1), adding[HEAD_SIZE:])
    yield query, local, map_low, map_high


def group_norm(wkv, gain, bias):
    centred = wkv - head_sum(wkv) * (1.0 / HEAD_SIZE)
    spread = head_sum(centred * centred) * (1.0 / HEAD_SIZE)
    return centred * lax.rsqrt(spread + 0.00064) * gain + bias


class Remote:
    def __init__(self):
        self.started = []

    def send(self, source, target, send, recv, device):
        copy = pltpu.make_async_remote_copy(
            src_ref=source,
            dst_ref=target,
            send_sem=send,
            recv_sem=recv,
            device_id=device,
            device_id_type=MESH,
        )
        copy.start()
        self.started.append(copy)
        return copy

    def drain(self):
        for copy in self.started:
            copy.wait_send()


def layer_kernel(
    tokens_hbm,
    token_mix,
    weights_hbm,
    downs_hbm,
    ups,
    vectors,
    output_hbm,
    out,
    wide,
    edge,
    weights,
    downs,
    output_weight,
    sums,
    low_sums,
    query,
    local,
    normed,
    maps,
    got,
    states,
    entry,
    part,
    mate_got,
    across,
    across_got,
    load_sem,
    own_sem,
    gather_send,
    gather_recv,
    pass_send,
    pass_recv,
    edge_send,
    edge_recv,
    map_send,
    map_recv,
    state_send,
    state_recv,
    mate_send,
    mate_recv,
    across_send,
    across_recv,
):
    n = lax.axis_size("seq")
    me = lax.axis_index("seq")
    peers = lax.axis_size("head")
    place = lax.axis_index("head")
    chips = peers // 2
    chip, core = place // 2, place % 2
    mate = chip * 2 + 1 - core
    _, seqs, size, own = wide.shape
    width = local.shape[1]
    heads = width // HEAD_SIZE
    slots = maps.shape[0]
    edge_rows = edge.shape[2]
    remote = Remote()

    def row_of(which, lanes):
        return vectors[which][lanes].reshape(1, PAIR)

    def at(seq, head):
        return {"seq": seq, "head": head}

    loads = []
    sources = list(weights_hbm) + list(downs_hbm) + [output_hbm]
    targets = list(weights) + list(downs) + [output_weight]
    own_copy = pltpu.make_async_copy(tokens_hbm, wide.at[place], own_sem.at[0])
    own_copy.start()
    for i, (source, target) in enumerate(zip(sources, targets)):
        copy = pltpu.make_async_copy(source, target, load_sem.at[i])
        copy.start()
        loads.append(copy)

    barrier = pltpu.get_barrier_semaphore()

    def greet(seq, head):
        pl.semaphore_signal(barrier, inc=1, device_id=at(seq, head), device_id_type=MESH)

    before, after = lax.rem(me + n - 1, n), lax.rem(me + 1, n)
    for d in range(1, n):
        greet(lax.rem(me + d, n), place)
    greet(me, mate)
    for d in range(1, chips):
        greet(me, lax.rem(chip + d, chips) * 2 + core)
    for d in range(1, peers):
        greet(before, lax.rem(place + d, peers))
    pl.semaphore_wait(barrier, n - 1 + chips + peers - 1)

    edges = {}

    def send_edge(d, swap):
        to_core = 1 - core if swap else core
        edges[d, swap] = remote.send(
            tokens_hbm.at[:, pl.ds(size - edge_rows, edge_rows), :],
            edge.at[place],
            edge_send.at[2 * d + swap],
            edge_recv.at[2 * d + swap],
            at(after, lax.rem(chip + d, chips) * 2 + to_core),
        )

    send_edge(0, 0)
    send_edge(0, 1)
    from_across = []
    for s in range(seqs):
        for d in range(1, chips):
            copy = remote.send(
                tokens_hbm.at[s],
                wide.at[place, s],
                gather_send.at[d, s],
                gather_recv.at[d, s],
                at(me, lax.rem(chip + d, chips) * 2 + core),
            )
            from_across.append((s, d, copy))
    from_mate = []
    for s in range(seqs):
        from_mate.append(
            remote.send(
                tokens_hbm.at[s],
                wide.at[place, s],
                gather_send.at[0, s],
                gather_recv.at[0, s],
                at(me, mate),
            )
        )
    for d in range(1, chips):
        send_edge(d, 0)
        send_edge(d, 1)
    maps[...] = jnp.zeros_like(maps)
    started = (me > 0).astype(F32)

    def absorb(h, initial):
        if len(token_mix.shape) == 3:
            mixing = token_mix[h]
        else:
            mixing = token_mix[:, pl.ds(pl.multiple_of(h * own, own), own)]
        currents, changes = [], []
        for s in range(seqs):
            current = wide[h, s].astype(F32)
            row = edge[h, s].astype(F32)[edge_rows - 1 :, :] * started
            earlier = jnp.where(iota(current.shape, 0) == 0, row, pltpu.roll(current, 1, 0))
            currents.append(current)
            changes.append(earlier - current)
        current = jnp.concatenate(currents, axis=0)
        change = jnp.concatenate(changes, axis=0)
        rows = pl.ds(pl.multiple_of(h * own, own), own)
        for j, total, weight in (
            (0, sums[0], weights[0]),
            (2, sums[1], weights[1]),
            (3, sums[2], weights[2]),
            (1, low_sums[0], downs[0]),
            (4, low_sums[1], downs[1]),
        ):
            blended = (current + change * mixing[j : j + 1, :]).astype(BF16)
            if j in (0, 2, 3):
                term = dot(blended, weight[rows, :])
            elif len(weight.shape) == 3:
                term = dot_nt(blended, weight[h])
            else:
                term = dot_nt(blended, weight[:, pl.ds(pl.multiple_of(h * own, own), own)])
            total[...] = term if initial else total[...] + term

    own_copy.wait()
    for copy in loads[:-1]:
        copy.wait()
    edges[0, 0].wait_recv()
    absorb(place, True)
    for copy in from_mate:
        copy.wait_recv()
    edges[0, 1].wait_recv()
    absorb(mate, False)
    passed = []
    for s, d, copy in from_across:
        copy.wait_recv()
        came = lax.rem(chip + chips - d, chips) * 2 + core
        passed.append(
            remote.send(
                wide.at[came, s],
                wide.at[came, s],
                pass_send.at[d, s],
                pass_recv.at[d, s],
                at(me, mate),
            )
        )
    for d in range(1, chips):
        edges[d, 0].wait_recv()
        absorb(lax.rem(chip + chips - d, chips) * 2 + core, False)
    for copy in passed:
        copy.wait_recv()
    for d in range(1, chips):
        edges[d, 1].wait_recv()
        absorb(lax.rem(chip + chips - d, chips) * 2 + 1 - core, False)

    masks = link_masks(size)

    def one(s):
        at_rows = pl.ds(s * size, size)
        decay_hidden = jnp.tanh(low_sums[0][at_rows, :]).astype(BF16)
        learn_hidden = low_sums[1][at_rows, :].astype(BF16)
        units = []
        for g in range(width // PAIR):
            lanes = pl.ds(g * PAIR, PAIR)
            units.append(
                chunk_maps(
                    masks,
                    sums[0][at_rows, lanes],
                    sums[1][at_rows, lanes],
                    sums[2][at_rows, lanes],
                    row_of(0, lanes) + dot(decay_hidden, ups[0][:, lanes]),
                    row_of(1, lanes) + dot(learn_hidden, ups[1][:, lanes]),
                    row_of(2, lanes),
                    row_of(3, lanes),
                )
            )
        for g, (q, rest, low, high) in enumerate(interleaved(units)):
            lanes = pl.ds(g * PAIR, PAIR)
            query[at_rows, lanes] = q.astype(BF16)
            local[at_rows, lanes] = rest
            pair = s * heads + 2 * g
            maps[pair // n, pair % n] = low.astype(BF16)
            maps[(pair + 1) // n, (pair + 1) % n] = high.astype(BF16)

    early = heads // n
    groups = [(0, early), (early, slots)] if early else [(0, slots)]

    def exchange(group, source, target, send, recv):
        low, high = groups[group]
        some = pl.ds(low, high - low)
        copies = []
        for d in range(1, n):
            there = lax.rem(me + d, n)
            copies.append(
                remote.send(
                    source.at[some, there],
                    target.at[some, me],
                    send.at[group, d],
                    recv.at[group, d],
                    at(there, place),
                )
            )
        for slot in range(low, high):
            target[slot, me] = source[slot, me]
        return copies

    pick = (iota((HEAD_SIZE, PAIR), 0) == iota((HEAD_SIZE, PAIR), 1)).astype(BF16)
    first = iota((HEAD_SIZE, PAIR), 1) < HEAD_SIZE

    def scan(group):
        members = range(*groups[group])
        packed = {slot: jnp.zeros((HEAD_SIZE, PAIR), BF16) for slot in members}
        for i in range(n):
            for slot in members:
                states[slot, i] = packed[slot]
            if i == n - 1:
                break
            for slot in members:
                follow = dot(got[slot, i], jnp.concatenate([packed[slot], pick], axis=0))
                whole = follow + pltpu.roll(follow, HEAD_SIZE, 1)
                coarse = whole.astype(BF16)
                fine = (whole - coarse.astype(F32)).astype(BF16)
                packed[slot] = jnp.where(first, coarse, fine)

    arriving = {}
    for s in range(seqs):
        one(s)
        if s == 0 and early:
            arriving[0] = exchange(0, maps, got, map_send, map_recv)
    last = len(groups) - 1
    arriving[last] = exchange(last, maps, got, map_send, map_recv)
    returning = []
    for group in range(len(groups)):
        for copy in arriving[group]:
            copy.wait_recv()
        scan(group)
        returning += exchange(group, states, entry, state_send, state_recv)
    for copy in returning:
        copy.wait_recv()

    def finish(s):
        at_rows = pl.ds(s * size, size)
        for g in range(width // PAIR):
            lanes = pl.ds(g * PAIR, PAIR)
            pair = s * heads + 2 * g
            low = entry[pair // n, pair % n]
            high = entry[(pair + 1) // n, (pair + 1) % n]
            zero = jnp.zeros_like(low)
            shifted = jnp.concatenate([zero[:, :HEAD_SIZE], high[:, :HEAD_SIZE]], axis=1)
            both = jnp.concatenate([jnp.where(first, low, zero), shifted], axis=0)
            wkv = local[at_rows, lanes] + dot(query[at_rows, lanes], both)
            normed[at_rows, lanes] = group_norm(
                wkv, row_of(4, lanes), row_of(5, lanes)
            ).astype(BF16)

    def columns(index):
        if len(output_weight.shape) == 3:
            return output_weight[index]
        return output_weight[:, pl.ds(pl.multiple_of(index * own, own), own)]

    loads[-1].wait()
    order = list(range(1, chips)) + [0]
    to_mate = {}
    for s in range(seqs):
        finish(s)
        at_rows = pl.ds(s * size, size)
        for d in order:
            other = lax.rem(chip + d, chips)
            part[d, s] = dot(normed[at_rows, :], columns(other * 2 + 1 - core)).astype(BF16)
            to_mate[d, s] = remote.send(
                part.at[d, s],
                mate_got.at[d, s],
                mate_send.at[d, s],
                mate_recv.at[d, s],
                at(me, mate),
            )
        for d in order[:-1]:
            other = lax.rem(chip + d, chips)
            mine = dot(normed[at_rows, :], columns(other * 2 + core))
            to_mate[d, s].wait_recv()
            across[d, s] = (mine + mate_got[d, s].astype(F32)).astype(BF16)
            to_mate[d, s, "far"] = remote.send(
                across.at[d, s],
                across_got.at[d, s],
                across_send.at[d, s],
                across_recv.at[d, s],
                at(me, other * 2 + core),
            )
    for s in range(seqs):
        at_rows = pl.ds(s * size, size)
        mine = dot(normed[at_rows, :], columns(place))
        to_mate[0, s].wait_recv()
        mine = mine + mate_got[0, s].astype(F32)
        for d in order[:-1]:
            to_mate[d, s, "far"].wait_recv()
            mine = mine + across_got[d, s].astype(F32)
        out[at_rows, :] = mine.astype(BF16)
    remote.drain()


def layer(tokens, token_mix, weights, downs, ups, vectors, output_weight):
    seqs, size, own = tokens.shape
    rows, width = seqs * size, weights[0].shape[1]
    n, peers = lax.axis_size("seq"), lax.axis_size("head")
    chips = peers // 2
    slots = -(-(seqs * width // HEAD_SIZE) // n)
    edge_rows = min(16, size)
    sems = pltpu.SemaphoreType.DMA
    table = pltpu.VMEM((slots, n, HEAD_SIZE, PAIR), BF16)
    piece = pltpu.VMEM((chips, seqs, size, own), BF16)
    inside = pl.BlockSpec(memory_space=pltpu.VMEM)
    outside = pl.BlockSpec(memory_space=pl.ANY)

    def like(array):
        return pltpu.VMEM(array.shape, array.dtype)

    return pl.pallas_call(
        layer_kernel,
        out_shape=jax.ShapeDtypeStruct((rows, own), BF16),
        in_specs=[outside, inside, [outside] * 3, [outside] * 2, [inside] * 2, [inside] * 6, outside],
        out_specs=inside,
        scratch_shapes=[
            pltpu.VMEM((peers, seqs, size, own), BF16),
            pltpu.VMEM((peers, seqs, edge_rows, own), BF16),
            [like(weight) for weight in weights],
            [like(down) for down in downs],
            like(output_weight),
            [pltpu.VMEM((rows, width), F32)] * 3,
            [pltpu.VMEM((rows, down.shape[-2]), F32) for down in downs],
            pltpu.VMEM((rows, width), BF16),
            pltpu.VMEM((rows, width), F32),
            pltpu.VMEM((rows, width), BF16),
            table,
            table,
            table,
            table,
            piece,
            piece,
            piece,
            piece,
            sems((len(weights) + len(downs) + 1,)),
            sems((1,)),
            sems((chips, seqs)),
            sems((chips, seqs)),
            sems((chips, seqs)),
            sems((chips, seqs)),
            sems((peers,)),
            sems((peers,)),
            sems((2, n)),
            sems((2, n)),
            sems((2, n)),
            sems((2, n)),
            sems((chips, seqs)),
            sems((chips, seqs)),
            sems((chips, seqs)),
            sems((chips, seqs)),
        ],
        compiler_params=pltpu.CompilerParams(
            collective_id=0, has_side_effects=True, vmem_limit_bytes=56 * 2**20
        ),
    )(tokens, token_mix, weights, downs, ups, vectors, output_weight)


def body(
    tokens,
    token_mix,
    receptance,
    key_weight,
    value_weight,
    decay_base,
    decay_down_matrix,
    decay_up_matrix,
    learn_base,
    learning_down_matrix,
    learning_up_matrix,
    key_scale,
    key_blend,
    norm_gain,
    norm_bias,
    output_weight,
):
    seqs, length, own_width = tokens.shape
    lack = -own_width % PAIR
    if lack:
        wider = lambda array: jnp.pad(array, [(0, 0)] * (array.ndim - 1) + [(0, lack)])
        receptance, key_weight, value_weight, decay_up_matrix, learning_up_matrix = map(
            wider, (receptance, key_weight, value_weight, decay_up_matrix, learning_up_matrix)
        )
        decay_base, learn_base, key_scale, key_blend, norm_gain, norm_bias = map(
            wider, (decay_base, learn_base, key_scale, key_blend, norm_gain, norm_bias)
        )
        output_weight = jnp.pad(output_weight, [(0, lack), (0, 0)])
        output_weight = output_weight.reshape(own_width + lack, -1, own_width).transpose(1, 0, 2)
        token_mix = token_mix.reshape(token_mix.shape[0], -1, own_width).transpose(1, 0, 2)
    downs = [decay_down_matrix.T, learning_down_matrix.T]
    if lack:
        downs = [down.reshape(down.shape[0], -1, own_width).transpose(1, 0, 2) for down in downs]
    vectors = [decay_base, learn_base, key_scale, key_blend, norm_gain, norm_bias]
    result = layer(
        tokens,
        token_mix,
        [receptance, key_weight, value_weight],
        downs,
        [decay_up_matrix, learning_up_matrix],
        vectors,
        output_weight,
    )
    return result.reshape(seqs, length, own_width)


def solution(mesh):
    placed = (
        P(None, "seq", "head"),
        P(),
        P(None, "head"),
        P(None, "head"),
        P(None, "head"),
        P("head"),
        P(),
        P(None, "head"),
        P("head"),
        P(),
        P(None, "head"),
        P("head"),
        P("head"),
        P("head"),
        P("head"),
        P("head", None),
    )
    return jax.shard_map(
        body, mesh=mesh, in_specs=placed, out_specs=P(None, "seq", "head"), check_vma=False
    )
```

```python
import math

import jax
import jax.numpy as jnp
from jax import lax
from jax.experimental import pallas as pl
from jax.experimental.pallas import tpu as pltpu
from jax.sharding import PartitionSpec as P

HEAD_SIZE = 64
PAIR = 2 * HEAD_SIZE
MESH = pl.DeviceIdType.MESH
F32 = jnp.float32
BF16 = jnp.bfloat16
DECAY_SCALE = math.exp(-0.5)


def dot(left, right):
    return jnp.dot(left, right, preferred_element_type=F32)


def dot_nt(left, right):
    return lax.dot_general(left, right, (((1,), (1,)), ((), ())), preferred_element_type=F32)


def dot_tn(left, right):
    return lax.dot_general(left, right, (((0,), (0,)), ((), ())), preferred_element_type=F32)


def iota(shape, axis):
    return lax.broadcasted_iota(jnp.int32, shape, axis)


def head_sum(values):
    first = iota(values.shape, 1) < HEAD_SIZE
    low = jnp.sum(jnp.where(first, values, 0.0), axis=-1, keepdims=True)
    high = jnp.sum(jnp.where(first, 0.0, values), axis=-1, keepdims=True)
    return jnp.where(first, low, high)


def diagonal(values):
    half = values.shape[1] // 2
    if half % PAIR == 0:
        zero = jnp.zeros_like(values[:, :half])
        upper = jnp.concatenate([values[:, :half], zero], axis=1)
        return jnp.concatenate(
            [upper, jnp.concatenate([zero, values[:, half:]], axis=1)], axis=0
        )
    first = iota(values.shape, 1) < half
    zero = jnp.zeros_like(values)
    return jnp.concatenate(
        [jnp.where(first, values, zero), jnp.where(first, zero, values)], axis=0
    )


def interleaved(units):
    while True:
        results = [next(unit) for unit in units]
        if results[0] is not None:
            return results


def link_masks(size):
    crossing = iota((size, 2 * size), 0) ^ (iota((size, 2 * size), 1) % size)
    blocks = [2**level for level in range((size - 1).bit_length())]
    return [((crossing >= b) & (crossing < 2 * b)).astype(F32).astype(BF16) for b in blocks]


def chunk_maps(masks, recept, key_raw, value, decay_arg, learn_arg, key_scale, key_blend):
    size = recept.shape[0]
    decay = -DECAY_SCALE / (1.0 + jnp.exp(-decay_arg))
    learn = 1.0 / (1.0 + jnp.exp(-learn_arg))
    scaled = key_raw * key_scale
    unit = scaled * lax.rsqrt(head_sum(scaled * scaled) + 1e-06)
    key = key_raw * (1.0 + (learn - 1.0) * key_blend)
    beta = unit * learn
    lower = (iota((size, size), 0) >= iota((size, size), 1)).astype(BF16)
    coarse = decay.astype(BF16)
    fine = (decay - coarse.astype(F32)).astype(BF16)
    sums = dot(lower, jnp.concatenate([coarse, fine], axis=1))
    yield
    cumul = sums[:, :PAIR] + sums[:, PAIR:]
    before = cumul - decay
    middle = cumul[size // 2 - 1 : size // 2, :]
    ending = cumul[size - 1 :, :]
    to_right = jnp.exp(middle - cumul)
    left = jnp.concatenate(
        [-unit * jnp.exp(before - middle), recept * jnp.exp(cumul - middle)], axis=0
    ).astype(BF16)
    with_beta = dot_nt(left, diagonal((beta * to_right).astype(BF16)))
    with_key = dot_nt(left, diagonal((key * to_right).astype(BF16)))
    yield
    row = iota((size, 2 * size), 0)
    column = iota((size, 2 * size), 1) % size
    strict = row > column
    within = row >= column
    lower_ab = jnp.where(strict, with_beta[:size], 0.0).astype(BF16)
    lower_ak = jnp.where(strict, with_key[:size], 0.0).astype(BF16)
    lower_rb = jnp.where(within, with_beta[size:], 0.0).astype(BF16)
    lower_rk = jnp.where(within, with_key[size:], 0.0).astype(BF16)
    inverse = jnp.where(row == column, 1.0, 0.0) + (lower_ab * masks[0]).astype(F32)
    for mask in masks[1:]:
        link = lower_ab * mask
        rounded = inverse.astype(BF16)
        half = dot(rounded, diagonal(link)).astype(BF16)
        yield
        inverse = inverse + dot(half, diagonal(rounded))
        yield
    yield
    value_b = value.astype(BF16)
    from_value = dot(jnp.concatenate([lower_ak, lower_rk], axis=0), diagonal(value_b))
    yield
    alpha_exp = (-unit * jnp.exp(before)).astype(BF16)
    gains = dot(
        inverse.astype(BF16),
        jnp.concatenate(
            [diagonal(alpha_exp), diagonal(from_value[:size].astype(BF16))], axis=1
        ),
    )
    yield
    gains_b = gains.astype(BF16)
    answers = dot(
        lower_rb,
        jnp.concatenate([diagonal(gains_b[:, :PAIR]), diagonal(gains_b[:, PAIR:])], axis=1),
    )
    yield
    query = recept * jnp.exp(cumul) + answers[:, :PAIR]
    local = from_value[size:] + answers[:, PAIR:]
    to_end = jnp.exp(ending - cumul)
    ends = jnp.concatenate([beta * to_end, key * to_end], axis=0)
    sources = jnp.concatenate(
        [gains_b, jnp.concatenate([jnp.zeros_like(value_b), value_b], axis=1)], axis=0
    )
    total = dot(jnp.transpose(ends).astype(BF16), sources)
    yield
    same = iota((PAIR, PAIR), 0) == iota((PAIR, PAIR), 1)
    moving = total[:, :PAIR] + jnp.where(same, jnp.exp(ending), 0.0)
    adding = total[:, PAIR:]
    first = iota((HEAD_SIZE, PAIR), 1) < HEAD_SIZE
    map_low = jnp.where(first, moving[:HEAD_SIZE], pltpu.roll(adding[:HEAD_SIZE], HEAD_SIZE, 1))
    map_high = jnp.where(first, pltpu.roll(moving[HEAD_SIZE:], HEAD_SIZE, 1), adding[HEAD_SIZE:])
    yield query, local, map_low, map_high


def group_norm(wkv, gain, bias):
    centred = wkv - head_sum(wkv) * (1.0 / HEAD_SIZE)
    spread = head_sum(centred * centred) * (1.0 / HEAD_SIZE)
    return centred * lax.rsqrt(spread + 0.00064) * gain + bias


class Remote:
    def __init__(self):
        self.started = []

    def send(self, source, target, send, recv, device):
        copy = pltpu.make_async_remote_copy(
            src_ref=source,
            dst_ref=target,
            send_sem=send,
            recv_sem=recv,
            device_id=device,
            device_id_type=MESH,
        )
        copy.start()
        self.started.append(copy)
        return copy

    def drain(self):
        for copy in self.started:
            copy.wait_send()


def layer_kernel(
    tokens_hbm,
    token_mix,
    weights_hbm,
    downs_hbm,
    ups,
    vectors,
    output_hbm,
    out,
    wide,
    edge,
    weights,
    downs,
    output_weight,
    sums,
    low_sums,
    query,
    local,
    normed,
    maps,
    got,
    states,
    entry,
    part,
    mate_got,
    across,
    across_got,
    load_sem,
    own_sem,
    gather_send,
    gather_recv,
    pass_send,
    pass_recv,
    edge_send,
    edge_recv,
    map_send,
    map_recv,
    state_send,
    state_recv,
    mate_send,
    mate_recv,
    across_send,
    across_recv,
):
    n = lax.axis_size("seq")
    me = lax.axis_index("seq")
    peers = lax.axis_size("head")
    place = lax.axis_index("head")
    chips = peers // 2
    chip, core = place // 2, place % 2
    mate = chip * 2 + 1 - core
    _, seqs, size, own = wide.shape
    width = local.shape[1]
    heads = width // HEAD_SIZE
    slots = maps.shape[0]
    edge_rows = edge.shape[2]
    remote = Remote()

    def row_of(which, lanes):
        return vectors[which][lanes].reshape(1, PAIR)

    def at(seq, head):
        return {"seq": seq, "head": head}

    loads = []
    sources = list(weights_hbm) + list(downs_hbm) + [output_hbm]
    targets = list(weights) + list(downs) + [output_weight]
    own_copy = pltpu.make_async_copy(tokens_hbm, wide.at[place], own_sem.at[0])
    own_copy.start()
    for i, (source, target) in enumerate(zip(sources, targets)):
        copy = pltpu.make_async_copy(source, target, load_sem.at[i])
        copy.start()
        loads.append(copy)

    barrier = pltpu.get_barrier_semaphore()

    def greet(seq, head):
        pl.semaphore_signal(barrier, inc=1, device_id=at(seq, head), device_id_type=MESH)

    before, after = lax.rem(me + n - 1, n), lax.rem(me + 1, n)
    for d in range(1, n):
        greet(lax.rem(me + d, n), place)
    greet(me, mate)
    for d in range(1, chips):
        greet(me, lax.rem(chip + d, chips) * 2 + core)
    for d in range(1, peers):
        greet(before, lax.rem(place + d, peers))
    pl.semaphore_wait(barrier, n - 1 + chips + peers - 1)

    edges = {}

    def send_edge(d, swap):
        to_core = 1 - core if swap else core
        edges[d, swap] = remote.send(
            tokens_hbm.at[:, pl.ds(size - edge_rows, edge_rows), :],
            edge.at[place],
            edge_send.at[2 * d + swap],
            edge_recv.at[2 * d + swap],
            at(after, lax.rem(chip + d, chips) * 2 + to_core),
        )

    send_edge(0, 0)
    send_edge(0, 1)
    from_across = []
    for s in range(seqs):
        for d in range(1, chips):
            copy = remote.send(
                tokens_hbm.at[s],
                wide.at[place, s],
                gather_send.at[d, s],
                gather_recv.at[d, s],
                at(me, lax.rem(chip + d, chips) * 2 + core),
            )
            from_across.append((s, d, copy))
    from_mate = []
    for s in range(seqs):
        from_mate.append(
            remote.send(
                tokens_hbm.at[s],
                wide.at[place, s],
                gather_send.at[0, s],
                gather_recv.at[0, s],
                at(me, mate),
            )
        )
    for d in range(1, chips):
        send_edge(d, 0)
        send_edge(d, 1)
    maps[...] = jnp.zeros_like(maps)
    started = (me > 0).astype(F32)

    def absorb(h, initial):
        if len(token_mix.shape) == 3:
            mixing = token_mix[h]
        else:
            mixing = token_mix[:, pl.ds(pl.multiple_of(h * own, own), own)]
        currents, changes = [], []
        for s in range(seqs):
            current = wide[h, s].astype(F32)
            row = edge[h, s].astype(F32)[edge_rows - 1 :, :] * started
            earlier = jnp.where(iota(current.shape, 0) == 0, row, pltpu.roll(current, 1, 0))
            currents.append(current)
            changes.append(earlier - current)
        current = jnp.concatenate(currents, axis=0)
        change = jnp.concatenate(changes, axis=0)
        rows = pl.ds(pl.multiple_of(h * own, own), own)
        for load, j, total, weight in (
            (loads[0], 0, sums[0], weights[0]),
            (loads[1], 2, sums[1], weights[1]),
            (loads[2], 3, sums[2], weights[2]),
            (loads[3], 1, low_sums[0], downs[0]),
            (loads[4], 4, low_sums[1], downs[1]),
        ):
            blended = (current + change * mixing[j : j + 1, :]).astype(BF16)
            if initial:
                load.wait()
            if j in (0, 2, 3):
                term = dot(blended, weight[rows, :])
            elif len(weight.shape) == 3:
                term = dot_nt(blended, weight[h])
            else:
                term = dot_nt(blended, weight[:, pl.ds(pl.multiple_of(h * own, own), own)])
            total[...] = term if initial else total[...] + term

    own_copy.wait()
    edges[0, 0].wait_recv()
    absorb(place, True)
    for copy in from_mate:
        copy.wait_recv()
    edges[0, 1].wait_recv()
    absorb(mate, False)
    passed = []
    for s, d, copy in from_across:
        copy.wait_recv()
        came = lax.rem(chip + chips - d, chips) * 2 + core
        passed.append(
            remote.send(
                wide.at[came, s],
                wide.at[came, s],
                pass_send.at[d, s],
                pass_recv.at[d, s],
                at(me, mate),
            )
        )
    for d in range(1, chips):
        edges[d, 0].wait_recv()
        absorb(lax.rem(chip + chips - d, chips) * 2 + core, False)
    for copy in passed:
        copy.wait_recv()
    for d in range(1, chips):
        edges[d, 1].wait_recv()
        absorb(lax.rem(chip + chips - d, chips) * 2 + 1 - core, False)

    masks = link_masks(size)

    def one(s):
        at_rows = pl.ds(s * size, size)
        decay_hidden = jnp.tanh(low_sums[0][at_rows, :]).astype(BF16)
        learn_hidden = low_sums[1][at_rows, :].astype(BF16)
        units = []
        for g in range(width // PAIR):
            lanes = pl.ds(g * PAIR, PAIR)
            units.append(
                chunk_maps(
                    masks,
                    sums[0][at_rows, lanes],
                    sums[1][at_rows, lanes],
                    sums[2][at_rows, lanes],
                    row_of(0, lanes) + dot(decay_hidden, ups[0][:, lanes]),
                    row_of(1, lanes) + dot(learn_hidden, ups[1][:, lanes]),
                    row_of(2, lanes),
                    row_of(3, lanes),
                )
            )
        for g, (q, rest, low, high) in enumerate(interleaved(units)):
            lanes = pl.ds(g * PAIR, PAIR)
            query[at_rows, lanes] = q.astype(BF16)
            local[at_rows, lanes] = rest
            pair = s * heads + 2 * g
            maps[pair // n, pair % n] = low.astype(BF16)
            maps[(pair + 1) // n, (pair + 1) % n] = high.astype(BF16)

    early = heads // n
    groups = [(0, early), (early, slots)] if early else [(0, slots)]

    def exchange(group, source, target, send, recv):
        low, high = groups[group]
        some = pl.ds(low, high - low)
        copies = []
        for d in range(1, n):
            there = lax.rem(me + d, n)
            copies.append(
                remote.send(
                    source.at[some, there],
                    target.at[some, me],
                    send.at[group, d],
                    recv.at[group, d],
                    at(there, place),
                )
            )
        for slot in range(low, high):
            target[slot, me] = source[slot, me]
        return copies

    pick = (iota((HEAD_SIZE, PAIR), 0) == iota((HEAD_SIZE, PAIR), 1)).astype(BF16)
    first = iota((HEAD_SIZE, PAIR), 1) < HEAD_SIZE

    def scan(group):
        members = range(*groups[group])
        packed = {slot: jnp.zeros((HEAD_SIZE, PAIR), BF16) for slot in members}
        for i in range(n):
            for slot in members:
                states[slot, i] = packed[slot]
            if i == n - 1:
                break
            for slot in members:
                follow = dot(got[slot, i], jnp.concatenate([packed[slot], pick], axis=0))
                whole = follow + pltpu.roll(follow, HEAD_SIZE, 1)
                coarse = whole.astype(BF16)
                fine = (whole - coarse.astype(F32)).astype(BF16)
                packed[slot] = jnp.where(first, coarse, fine)

    arriving = {}
    for s in range(seqs):
        one(s)
        if s == 0 and early:
            arriving[0] = exchange(0, maps, got, map_send, map_recv)
    last = len(groups) - 1
    arriving[last] = exchange(last, maps, got, map_send, map_recv)
    returning = []
    for group in range(len(groups)):
        for copy in arriving[group]:
            copy.wait_recv()
        scan(group)
        returning += exchange(group, states, entry, state_send, state_recv)
    for copy in returning:
        copy.wait_recv()

    def finish(s):
        at_rows = pl.ds(s * size, size)
        for g in range(width // PAIR):
            lanes = pl.ds(g * PAIR, PAIR)
            pair = s * heads + 2 * g
            low = entry[pair // n, pair % n]
            high = entry[(pair + 1) // n, (pair + 1) % n]
            zero = jnp.zeros_like(low)
            shifted = jnp.concatenate([zero[:, :HEAD_SIZE], high[:, :HEAD_SIZE]], axis=1)
            both = jnp.concatenate([jnp.where(first, low, zero), shifted], axis=0)
            wkv = local[at_rows, lanes] + dot(query[at_rows, lanes], both)
            normed[at_rows, lanes] = group_norm(
                wkv, row_of(4, lanes), row_of(5, lanes)
            ).astype(BF16)

    def columns(index):
        if len(output_weight.shape) == 3:
            return output_weight[index]
        return output_weight[:, pl.ds(pl.multiple_of(index * own, own), own)]

    loads[-1].wait()
    order = list(range(1, chips)) + [0]
    to_mate = {}
    for s in range(seqs):
        finish(s)
        at_rows = pl.ds(s * size, size)
        for d in order:
            other = lax.rem(chip + d, chips)
            part[d, s] = dot(normed[at_rows, :], columns(other * 2 + 1 - core)).astype(BF16)
            to_mate[d, s] = remote.send(
                part.at[d, s],
                mate_got.at[d, s],
                mate_send.at[d, s],
                mate_recv.at[d, s],
                at(me, mate),
            )
        for d in order[:-1]:
            other = lax.rem(chip + d, chips)
            mine = dot(normed[at_rows, :], columns(other * 2 + core))
            to_mate[d, s].wait_recv()
            across[d, s] = (mine + mate_got[d, s].astype(F32)).astype(BF16)
            to_mate[d, s, "far"] = remote.send(
                across.at[d, s],
                across_got.at[d, s],
                across_send.at[d, s],
                across_recv.at[d, s],
                at(me, other * 2 + core),
            )
    for s in range(seqs):
        at_rows = pl.ds(s * size, size)
        mine = dot(normed[at_rows, :], columns(place))
        to_mate[0, s].wait_recv()
        mine = mine + mate_got[0, s].astype(F32)
        for d in order[:-1]:
            to_mate[d, s, "far"].wait_recv()
            mine = mine + across_got[d, s].astype(F32)
        out[at_rows, :] = mine.astype(BF16)
    remote.drain()


def layer(tokens, token_mix, weights, downs, ups, vectors, output_weight):
    seqs, size, own = tokens.shape
    rows, width = seqs * size, weights[0].shape[1]
    n, peers = lax.axis_size("seq"), lax.axis_size("head")
    chips = peers // 2
    slots = -(-(seqs * width // HEAD_SIZE) // n)
    edge_rows = min(16, size)
    sems = pltpu.SemaphoreType.DMA
    table = pltpu.VMEM((slots, n, HEAD_SIZE, PAIR), BF16)
    piece = pltpu.VMEM((chips, seqs, size, own), BF16)
    inside = pl.BlockSpec(memory_space=pltpu.VMEM)
    outside = pl.BlockSpec(memory_space=pl.ANY)

    def like(array):
        return pltpu.VMEM(array.shape, array.dtype)

    return pl.pallas_call(
        layer_kernel,
        out_shape=jax.ShapeDtypeStruct((rows, own), BF16),
        in_specs=[outside, inside, [outside] * 3, [outside] * 2, [inside] * 2, [inside] * 6, outside],
        out_specs=inside,
        scratch_shapes=[
            pltpu.VMEM((peers, seqs, size, own), BF16),
            pltpu.VMEM((peers, seqs, edge_rows, own), BF16),
            [like(weight) for weight in weights],
            [like(down) for down in downs],
            like(output_weight),
            [pltpu.VMEM((rows, width), F32)] * 3,
            [pltpu.VMEM((rows, down.shape[-2]), F32) for down in downs],
            pltpu.VMEM((rows, width), BF16),
            pltpu.VMEM((rows, width), F32),
            pltpu.VMEM((rows, width), BF16),
            table,
            table,
            table,
            table,
            piece,
            piece,
            piece,
            piece,
            sems((len(weights) + len(downs) + 1,)),
            sems((1,)),
            sems((chips, seqs)),
            sems((chips, seqs)),
            sems((chips, seqs)),
            sems((chips, seqs)),
            sems((peers,)),
            sems((peers,)),
            sems((2, n)),
            sems((2, n)),
            sems((2, n)),
            sems((2, n)),
            sems((chips, seqs)),
            sems((chips, seqs)),
            sems((chips, seqs)),
            sems((chips, seqs)),
        ],
        compiler_params=pltpu.CompilerParams(
            collective_id=0, has_side_effects=True, vmem_limit_bytes=56 * 2**20
        ),
    )(tokens, token_mix, weights, downs, ups, vectors, output_weight)


def body(
    tokens,
    token_mix,
    receptance,
    key_weight,
    value_weight,
    decay_base,
    decay_down_matrix,
    decay_up_matrix,
    learn_base,
    learning_down_matrix,
    learning_up_matrix,
    key_scale,
    key_blend,
    norm_gain,
    norm_bias,
    output_weight,
):
    seqs, length, own_width = tokens.shape
    lack = -own_width % PAIR
    if lack:
        wider = lambda array: jnp.pad(array, [(0, 0)] * (array.ndim - 1) + [(0, lack)])
        receptance, key_weight, value_weight, decay_up_matrix, learning_up_matrix = map(
            wider, (receptance, key_weight, value_weight, decay_up_matrix, learning_up_matrix)
        )
        decay_base, learn_base, key_scale, key_blend, norm_gain, norm_bias = map(
            wider, (decay_base, learn_base, key_scale, key_blend, norm_gain, norm_bias)
        )
        output_weight = jnp.pad(output_weight, [(0, lack), (0, 0)])
        output_weight = output_weight.reshape(own_width + lack, -1, own_width).transpose(1, 0, 2)
        token_mix = token_mix.reshape(token_mix.shape[0], -1, own_width).transpose(1, 0, 2)
    downs = [decay_down_matrix.T, learning_down_matrix.T]
    if lack:
        downs = [down.reshape(down.shape[0], -1, own_width).transpose(1, 0, 2) for down in downs]
    vectors = [decay_base, learn_base, key_scale, key_blend, norm_gain, norm_bias]
    result = layer(
        tokens,
        token_mix,
        [receptance, key_weight, value_weight],
        downs,
        [decay_up_matrix, learning_up_matrix],
        vectors,
        output_weight,
    )
    return result.reshape(seqs, length, own_width)


def solution(mesh):
    placed = (
        P(None, "seq", "head"),
        P(),
        P(None, "head"),
        P(None, "head"),
        P(None, "head"),
        P("head"),
        P(),
        P(None, "head"),
        P("head"),
        P(),
        P(None, "head"),
        P("head"),
        P("head"),
        P("head"),
        P("head"),
        P("head", None),
    )
    return jax.shard_map(
        body, mesh=mesh, in_specs=placed, out_specs=P(None, "seq", "head"), check_vma=False
    )
```
